128 devices in a mesh: row: 16 (over y, x), col: 8 (over z, core).
Axes of the slice: x: 4, y: 4, z: 4, core: 2. Of those that a mesh axis runs over, the one named last changes fastest.
Arguments:
- tokens: bfloat16 [2048, 8192], P('row', 'col'), may hold values from -6 to 6
- weight: bfloat16 [8192, 28672], P('row', 'col'), may hold values from -0.0625 to 0.0625
- left_factors: bfloat16 [1024, 8192], P('row', 'col'), may hold values from -6 to 6
- right_factors: bfloat16 [1024, 28672], P('row', 'col'), may hold values from -6 to 6
- fitness: float32 [1024], P('row'), may hold values from -12 to 12
Outputs:
- outputs: bfloat16 [2048, 28672], P('row', 'col')
- update: bfloat16 [8192, 28672], P('row', 'col')
The draws below stay inside these ranges and needn't reach their ends.
All inputs are finite; a program needn't handle non-finite values.
Results may differ from the reference program's by a relative error of at most 0.005.
Values may be sent and summed in bfloat16 or wider, within the bound.
No kernel may reach another device: no remote copies, remote signals or barrier semaphores. Data moves between devices by JAX's collectives and lax.ppermute only.
A program may use at most 128 MiB of HBM per device.

```python
import math
import jax
import jax.numpy as jnp

D = 8192
FF = 28672
TOK_MEM = 2
MEMBERS = 1024
ROWS = 2048


def draw_fitness(key, part):
    key = jax.random.fold_in(key, 11)
    index = jnp.arange(MEMBERS, dtype=jnp.float32)
    scale = 1.0 + 2.0 * index / max(MEMBERS - 1, 1)
    values = jax.random.normal(key, (MEMBERS,), jnp.float32) * scale
    return jnp.clip(values, -12.0, 12.0).astype(jnp.float32)


def block_levels(key, extent, split, low, top_value):
    loudness, own = 1.0, jax.random.fold_in(key, 6)
    for axis_at, blocks in split:
        heights = jnp.exp(jax.random.uniform(jax.random.fold_in(own, axis_at), (blocks,), jnp.float32, low / len(split), top_value / len(split)))
        loudness = loudness * jnp.repeat(heights, extent[axis_at] // blocks).reshape([-1 if axis == axis_at else 1 for axis in range(len(extent))])
    return loudness


def normal_values(own_key, dims, deviation, bound, shards=(), kind=jnp.bfloat16):
    result = jax.random.normal(own_key, dims, jnp.float32) * deviation
    if len(shards) > 0:
        result = block_levels(own_key, dims, shards, -0.22, 0.18) * result
    return jnp.clip(result, min=-bound, max=bound).astype(kind)


def setup_inputs(seed: int = 0) -> dict:
    arg_keys = jax.random.split(jax.random.key(seed), 6)
    return {
        "tokens": normal_values(arg_keys[0], (ROWS, D), 1.0, 6.0, ((0, 16), (1, 8))),
        "weight": normal_values(arg_keys[1], (D, FF), D ** -0.5, 0.0625, ((0, 16), (1, 8))),
        "left_factors": normal_values(arg_keys[2], (MEMBERS, D), 1.0, 6.0, ((0, 16), (1, 8))),
        "right_factors": normal_values(arg_keys[3], (MEMBERS, FF), 1.0, 6.0, ((0, 16), (1, 8))),
        "fitness": draw_fitness(jax.random.fold_in(arg_keys[5], 71), 0),
    }


noise_scale = 0.5
epsilon = 1e-05

def reference(tokens, weight, left_factors, right_factors, fitness):
    base = jnp.dot(tokens, weight, preferred_element_type=jnp.float32)
    grouped = tokens.reshape(MEMBERS, TOK_MEM, D).astype(jnp.float32)
    probe = jnp.einsum('mtd,md->mt', grouped, left_factors.astype(jnp.float32)) / math.sqrt(D)
    perturbed = base.reshape(MEMBERS, TOK_MEM, FF) + noise_scale * probe[:, :, None] * right_factors.astype(jnp.float32)[:, None, :]
    outputs = perturbed.reshape(ROWS, FF).astype(jnp.bfloat16)
    mean = jnp.sum(fitness) / MEMBERS
    spread = jnp.sum((fitness - mean) * (fitness - mean)) / MEMBERS
    scores = (fitness - mean) / jnp.sqrt(spread + epsilon)
    weighted = (scores[:, None] * right_factors.astype(jnp.float32)).astype(jnp.bfloat16)
    total = jnp.dot(left_factors.T, weighted, preferred_element_type=jnp.float32)
    update = (total / math.sqrt(MEMBERS)).astype(jnp.bfloat16)
    return (outputs, update)
```

```python
import math

import jax
import jax.numpy as jnp
from jax import lax
from jax.sharding import Mesh, PartitionSpec as P

noise_scale = 0.5
epsilon = 1e-05


def shift(value, axis, by):
    return lax.ppermute(value, axis, [(i, (i + by) % 4) for i in range(4)])


def body(tokens, weight, left_factors, right_factors, fitness):
    y, x, z, c = (lax.axis_index(name) for name in ("y", "x", "z", "c"))
    members, width = left_factors.shape
    out_cols = weight.shape[1]
    quarter = out_cols // 4
    features = width * 8
    population = members * 16

    grouped = tokens.reshape(members, 2, width)
    share = jnp.einsum("mtd,md->mt", grouped, left_factors, preferred_element_type=jnp.float32)
    small = jnp.concatenate([fitness, share.reshape(-1)])
    small_all = lax.all_gather(small, ("y", "x", "z", "c"), axis=0, tiled=False)
    right_all = lax.all_gather(right_factors, ("y", "x"), axis=0, tiled=True)

    weight_x = lax.all_to_all(weight, "x", split_axis=1, concat_axis=0, tiled=True)

    both = jnp.concatenate(
        [tokens.reshape(4, -1, width), left_factors.reshape(4, -1, width)], axis=1
    )
    tok_rows = tokens.shape[0] // 4
    arrived = []
    for s in range(4):
        piece = lax.dynamic_index_in_dim(both, (y + s) % 4, 0, keepdims=False)
        perm = [(4 * yy + zz, 4 * zz + (yy + s) % 4) for yy in range(4) for zz in range(4)]
        arrived.append(lax.ppermute(piece, ("y", "z"), perm))
    arrived = jnp.stack(arrived)
    tok_y = arrived[:, :tok_rows].reshape(4 * tok_rows, width)
    left_y = arrived[:, tok_rows:].reshape(members, width)

    half = width // 2

    def left_for(xx):
        cols = lax.dynamic_slice_in_dim(left_y, (xx % 2) * half, half, 1)
        return jnp.concatenate([cols[: members // 2], cols[members // 2 :]], axis=1)

    slots = []
    for d in range(4):
        sent = jnp.concatenate([tok_y, left_for((x + d) % 4)], axis=0)
        slots.append(sent if d == 0 else shift(sent, "x", d))
    slots = jnp.stack(slots)
    tok_x = slots[:, : 4 * tok_rows].reshape(16 * tok_rows, width)
    left_x = slots[:, 4 * tok_rows :]
    left_x = jnp.concatenate([left_x[..., :half], left_x[..., half:]], axis=1)
    swap = [(0, 1), (1, 0)]
    left_o = lax.ppermute(left_x, "c", swap)
    left_x = jnp.where(c == x // 2, left_x, left_o)
    left_x = left_x.reshape(4 * members, half)
    mine = lax.dynamic_slice_in_dim(left_x, c * 2 * members, 2 * members, 0)
    mine = jnp.concatenate([mine[:members], mine[members:]], axis=1)

    ring = [(2 * zz, 2 * ((zz + 1) % 4)) for zz in range(4)]
    ring += [(2 * zz + 1, 2 * ((zz - 1) % 4) + 1) for zz in range(4)]
    held = [jnp.concatenate([tok_x, mine], axis=0)]
    for _ in range(3):
        held.append(lax.ppermute(held[-1], ("z", "c"), ring))
    other = [lax.ppermute(h, "c", swap) for h in held]
    low = [jnp.where(c == 0, h, o) for h, o in zip(held, other)]
    high = [jnp.where(c == 0, o, h) for h, o in zip(held, other)]
    rows = 16 * tok_rows

    def partial(k):
        top = jnp.dot(low[k][:rows], weight_x[:width], preferred_element_type=jnp.float32)
        bottom = jnp.dot(high[-k % 4][:rows], weight_x[width:], preferred_element_type=jnp.float32)
        return (top + bottom).astype(jnp.bfloat16).reshape(4, 4, tok_rows, quarter)

    sums = {}
    for pair in ((0, 2), (1, 3)):
        parts = [partial(k) for k in pair]

        def block(yy):
            return jnp.stack(
                [
                    lax.dynamic_index_in_dim(p, (z - k - yy) % 4, 1, keepdims=False)
                    for k, p in zip(pair, parts)
                ]
            )

        total = block(y).astype(jnp.float32)
        for dy in range(1, 4):
            total = total + shift(block((y + dy) % 4), "y", dy).astype(jnp.float32)
        for i, k in enumerate(pair):
            sums[k] = total[i].astype(jnp.bfloat16)
    summed = jnp.stack([sums[k] for k in range(4)])
    columns = []
    for d in range(4):
        sent = summed[:, d]
        columns.append(sent if d == 0 else shift(sent, "x", -d))
    columns = jnp.stack(columns)
    columns = jnp.stack([lax.dynamic_index_in_dim(columns, (z - zz) % 4, 1, keepdims=False) for zz in range(4)], 1)
    base = jnp.concatenate(
        [
            lax.dynamic_index_in_dim(columns, (q - x) % 4, 0, keepdims=False).reshape(4 * tok_rows, quarter)
            for q in range(4)
        ],
        axis=1,
    )

    shares = lax.dynamic_slice_in_dim(small_all, (4 * y + x) * 8, 8, 0)[:, members:]
    probe = jnp.sum(shares, axis=0).reshape(members, 2) / math.sqrt(features)
    fit = small_all.reshape(16, 8, -1)[:, 0, :members].reshape(-1)
    outputs = (
        base.astype(jnp.float32).reshape(members, 2, out_cols)
        + noise_scale * probe[:, :, None] * right_factors.astype(jnp.float32)[:, None, :]
    )
    outputs = outputs.reshape(2 * members, out_cols).astype(jnp.bfloat16)

    mean = jnp.sum(fit) / population
    centred = fit - mean
    scores = centred / jnp.sqrt(jnp.sum(centred * centred) / population + epsilon)
    weighted = (scores[:, None] * right_all.astype(jnp.float32)).astype(jnp.bfloat16)

    def left_half(h):
        v = h[rows:]
        return jnp.concatenate([v[:, :half], v[:, half:]], axis=0).reshape(2, 4, members // 4, half)

    by_z = [
        jnp.concatenate([left_half(low[k]), left_half(high[-k % 4])], axis=0) for k in range(4)
    ]
    by_z = jnp.stack(by_z)
    blocks = []
    for zz in range(4):
        blocks.append(lax.dynamic_index_in_dim(by_z, (z - zz) % 4, 0, keepdims=False))
    blocks = jnp.stack(blocks)
    blocks = jnp.stack(
        [lax.dynamic_index_in_dim(blocks, (x - xx) % 4, 1, keepdims=False) for xx in range(4)], 1
    )
    ordered = []
    for yy in range(4):
        ordered.append(jnp.stack([blocks[zz, :, (zz - yy) % 4] for zz in range(4)], 1))
    left_all = jnp.stack(ordered).reshape(population, half)
    total = lax.dot_general(
        left_all, weighted, (((0,), (0,)), ((), ())), preferred_element_type=jnp.float32
    )
    update = (total / math.sqrt(population)).astype(jnp.bfloat16)
    return outputs, update


def solution(mesh):
    grid = Mesh(mesh.devices.reshape(4, 4, 4, 2), ("y", "x", "z", "c"))
    spec = P(("y", "x"), ("z", "c"))
    return jax.shard_map(
        body,
        mesh=grid,
        in_specs=(spec, spec, spec, spec, P(("y", "x"))),
        out_specs=(spec, spec),
        check_vma=False,
    )
```

```python
import math

import jax
import jax.numpy as jnp
from jax import lax
from jax.experimental import pallas as pl
from jax.experimental.pallas import tpu as pltpu
from jax.sharding import Mesh, PartitionSpec as P

noise_scale = 0.5
epsilon = 1e-05
F32, BF16 = jnp.float32, jnp.bfloat16
VMEM = 48 * 2**20
SWAP = [(0, 1), (1, 0)]


def shift(value, axis, by):
    return lax.ppermute(value, axis, [(i, (i + by) % 4) for i in range(4)])


def apart(value, axis, up, down):
    perm = [(2 * i, 2 * ((i + up) % 4)) for i in range(4)]
    perm += [(2 * i + 1, 2 * ((i + down) % 4) + 1) for i in range(4)]
    return lax.ppermute(value, (axis, "c"), perm)


def after(value, *others):
    return lax.optimization_barrier((value, *others))[0]


def together(*values):
    return lax.optimization_barrier(values)


def pick(value, index):
    return lax.dynamic_index_in_dim(value, index, 0, keepdims=False)


def whole(shape):
    return pl.BlockSpec(shape, lambda i, s: (0,) * len(shape))


def base_kernel(s_ref, own0, other0, own1, other1, mine, near, far, across0, across1, *out_refs):
    nx, _, rows, _ = out_refs[0].shape
    ny = len(out_refs)
    depth = mine.shape[0]
    x, c = s_ref[1], s_ref[3]
    away = jnp.where(c == 0, 1, -1)
    low = depth // 2
    for k, (own, other) in enumerate(((own0, other0), (own1, other1))):
        total = None
        for piece, by, skip in (
            (mine, 0, 0), (near, -away, 0), (far, away, 0), (across0, 2, 0), (across1, 2, low)
        ):
            block = lax.rem(x + by + 4, 4)
            at = pl.ds(pl.multiple_of(lax.rem(block, 2) * depth + skip, 128), piece.shape[0])
            tok = jnp.where(lax.div(block, 2) == c, own[:, at], other[:, at])
            term = jnp.dot(tok, piece[...], preferred_element_type=F32)
            total = term if total is None else total + term
        total = total.astype(BF16)
        for d in range(nx):
            parts = [total[(d * ny + s) * rows : (d * ny + s + 1) * rows] for s in range(ny)]
            out_refs[0][d, k] = jnp.where(c == 0, parts[1], parts[3])
            out_refs[1][d, k] = parts[2]
            out_refs[2][d, k] = jnp.where(c == 0, parts[3], parts[1])
            out_refs[3][d, k] = parts[0]


def base_part(place, own0, other0, own1, other1, weight, moved):
    depth, cols = moved[0].shape
    height, width = own0.shape
    rows = height // 16
    return pl.pallas_call(
        base_kernel,
        grid_spec=pltpu.PrefetchScalarGridSpec(
            num_scalar_prefetch=1,
            grid=(1,),
            in_specs=[whole((height, width))] * 4
            + [pl.BlockSpec((depth, cols), lambda i, s: (0, s[1]))]
            + [whole(m.shape) for m in moved],
            out_specs=[whole((4, 2, rows, cols))] * 4,
        ),
        out_shape=[jax.ShapeDtypeStruct((4, 2, rows, cols), BF16)] * 4,
        compiler_params=pltpu.CompilerParams(vmem_limit_bytes=VMEM),
        cost_estimate=pl.CostEstimate(
            flops=16 * height * depth * cols,
            bytes_accessed=16 * height * depth + 4 * height * cols + 8 * depth * cols,
            transcendentals=0,
        ),
        name="base",
    )(place, own0, other0, own1, other1, weight, *moved)


def output_kernel(s_ref, sums_ref, probe_ref, right_ref, out_ref):
    z, c = s_ref[2], s_ref[3]
    rows = sums_ref.shape[2]
    members = right_ref.shape[0]
    row = lax.broadcasted_iota(jnp.int32, (2 * members, members), 0)
    member = lax.broadcasted_iota(jnp.int32, (2 * members, members), 1)
    twice = jnp.where(lax.div(row, 2) == member, 1.0, 0.0).astype(BF16)
    right = jnp.dot(twice, right_ref[...], preferred_element_type=F32)
    for zz in range(4):
        k = lax.rem(jnp.where(c == 0, z - zz, zz - z) + 4, 4)
        at = slice(zz * rows, (zz + 1) * rows)
        out = sums_ref[0, lax.rem(k, 2) * 2 + lax.div(k, 2)].astype(F32)
        out_ref[at] = (out + probe_ref[at] * right[at]).astype(BF16)


def output_part(place, sums, probe, right):
    _, _, rows, cols = sums.shape
    members = right.shape[0]
    return pl.pallas_call(
        output_kernel,
        grid_spec=pltpu.PrefetchScalarGridSpec(
            num_scalar_prefetch=1,
            grid=(4,),
            in_specs=[
                pl.BlockSpec((1, 4, rows, cols), lambda i, s: (lax.rem(i - s[1] + 4, 4), 0, 0, 0)),
                whole((4 * rows, 1)),
                pl.BlockSpec((members, cols), lambda i, s: (0, i)),
            ],
            out_specs=pl.BlockSpec((4 * rows, cols), lambda i, s: (0, i)),
        ),
        out_shape=jax.ShapeDtypeStruct((4 * rows, 4 * cols), BF16),
        compiler_params=pltpu.CompilerParams(vmem_limit_bytes=VMEM),
        name="outputs",
    )(place, sums, probe, right)


def update_kernel(s_ref, left0, left1, left2, left3, left_other, *refs):
    rights, fits = refs[:4], refs[4:8]
    out_ref, ordered, turned, scores = refs[-4:]
    population, cols = ordered.shape
    depth = population // 4

    @pl.when(pl.program_id(0) == 0)
    def _():
        z, c = s_ref[2], s_ref[3]
        count = population // 64
        for k, left in enumerate((left0, left1, left2, left3)):
            zz = lax.rem(jnp.where(c == 0, z - k, z + k) + 4, 4)
            for p in range(2):
                first = 2 * (c if p == 0 else 1 - c)
                for dd in range(2):
                    d = first + dd
                    d = jnp.where(c == 0, d, lax.rem(4 - d, 4))
                    for s in range(4):
                        slot = d * 4 + jnp.where(c == 0, s, -s % 4)
                        at = pl.multiple_of((slot * 4 + zz) * count, count)
                        rows, lanes = slice(s * count, (s + 1) * count), slice(dd * cols, (dd + 1) * cols)
                        ordered[pl.ds(at, count)] = left[rows, lanes] if p == 0 else left_other[-k % 4, rows, lanes]
        turned[...] = ordered[...].T
        fit = jnp.concatenate([f[...].astype(F32) for f in fits], axis=0)
        fit = fit[:, 0:1] + fit[:, 1:2] + fit[:, 2:3]
        mean = jnp.sum(fit, axis=0, keepdims=True) / population
        centred = fit - mean
        spread = jnp.sum(centred * centred, axis=0, keepdims=True) / population
        scores[...] = centred / jnp.sqrt(spread + epsilon)

    total = jnp.zeros(out_ref.shape, F32)
    for i in range(4):
        at = slice(i * depth, (i + 1) * depth)
        weighted = (scores[at] * rights[i][...].astype(F32)).astype(BF16)
        total += jnp.dot(turned[:, at], weighted, preferred_element_type=F32)
    out_ref[...] = (total * (1.0 / math.sqrt(population))).astype(BF16)


def update_part(place, left, left_other, rights, fits, fit_at, out_cols, first, cols, so_far=None):
    block = rights[0].shape[0]
    population = 4 * block
    depth = left[0].shape[1] // 2
    tile = 512
    extra = [] if so_far is None else [so_far]
    inputs = [*left, left_other, *rights, *fits, *extra]
    return pl.pallas_call(
        update_kernel,
        grid_spec=pltpu.PrefetchScalarGridSpec(
            num_scalar_prefetch=1,
            grid=(cols // tile,),
            in_specs=[whole(left[0].shape)] * 4
            + [whole(left_other.shape)]
            + [pl.BlockSpec((block, tile), lambda i, s: (0, i))] * 4
            + [pl.BlockSpec((block, 128), lambda i, s: (0, fit_at // 128))] * 4
            + [pl.BlockSpec(memory_space=pl.ANY)] * len(extra),
            out_specs=pl.BlockSpec((depth, tile), lambda i, s: (0, i + first // tile)),
            scratch_shapes=[
                pltpu.VMEM((population, depth), BF16),
                pltpu.VMEM((depth, population), BF16),
                pltpu.VMEM((population, 1), F32),
            ],
        ),
        out_shape=jax.ShapeDtypeStruct((depth, out_cols), BF16),
        input_output_aliases={len(inputs): 0} if extra else {},
        compiler_params=pltpu.CompilerParams(vmem_limit_bytes=VMEM),
        cost_estimate=pl.CostEstimate(
            flops=2 * population * depth * cols,
            bytes_accessed=2 * (population * (cols + depth) + depth * cols),
            transcendentals=0,
        ),
        name="update",
    )(place, *inputs)


def pieces(value):
    out = []
    for _ in range(3):
        top = lax.reduce_precision(value, 8, 7)
        out.append(top.astype(BF16))
        value = value - top
    return out


def body(tokens, weight, left_factors, right_factors, fitness):
    y, x, z, c = (lax.axis_index(name) for name in ("y", "x", "z", "c"))
    place = jnp.stack([y, x, z, c]).astype(jnp.int32)
    members, width = left_factors.shape
    depth, out_cols = weight.shape
    quarter = out_cols // 4
    features = width * 8
    population = members * 16
    rows = tokens.shape[0] // 4

    half = width // 2

    first = 4 * (out_cols // 7)
    beside = jnp.stack(pieces(fitness), axis=1)
    beside = jnp.pad(beside, ((0, 0), (0, 128 - beside.shape[1])))
    right = [jnp.concatenate([right_factors[:, :first], beside, right_factors[:, first:]], axis=1)]

    away = jnp.where(c == 0, 1, -1)

    def cols_of(source, xx):
        return lax.dynamic_slice_in_dim(source, (xx % 4) * quarter, quarter, 1)

    both = jnp.concatenate(
        [tokens.reshape(4, rows, width), left_factors.reshape(4, members // 4, width)], axis=1
    )
    own = pick(both, z)
    by_z = [own] + [shift(pick(both, (z + d) % 4), "z", d) for d in range(1, 4)]
    by_z = jnp.stack(by_z)
    near = apart(cols_of(after(weight, own), x + away), "x", 1, -1)
    by_z, weight, right[0] = together(by_z, weight, right[0])

    by_y = [pick(by_z, (z - y) % 4)] + [shift(pick(by_z, (z - y - d) % 4), "y", d) for d in range(1, 4)]
    by_y = jnp.stack(by_y)
    far = apart(cols_of(weight, x - away), "x", -1, 1)
    by_y, near, weight, right[0] = together(by_y, near, weight, right[0])

    tok_y = by_y[:, :rows].reshape(4 * rows, width)
    left_y = by_y[:, rows:].reshape(members, width)

    def left_for(xx):
        cols = lax.dynamic_slice_in_dim(left_y, (xx % 2) * half, half, 1)
        return jnp.concatenate([cols[: members // 2], cols[members // 2 :]], axis=1)

    slots = []
    for d in range(4):
        sent = jnp.concatenate([tok_y, left_for((x + d) % 4)], axis=0)
        slots.append(sent if d == 0 else shift(sent, "x", d))
    slots = jnp.stack(slots)
    right.append(apart(right[-1], "y", 1, -1))
    share = jnp.einsum(
        "mtd,md->mt", tokens.reshape(members, 2, width), left_factors, preferred_element_type=F32
    ).reshape(1, 2 * members)
    slots, far, share, right[1], weight = together(slots, far, share, right[1], weight)

    held = [slots[:, : 4 * rows].reshape(16 * rows, width)]
    held.append(apart(held[0], "z", 1, -1))
    other = [lax.ppermute(held[0], "c", SWAP)]
    across = cols_of(weight, x + 2)
    across = [apart(across[: depth // 2], "x", 2, 2), across[depth // 2 :]]
    right.append(apart(right[-1], "y", 1, -1))
    left_x = slots[:, 4 * rows :]
    left_x = jnp.concatenate([left_x[..., :half], left_x[..., half:]], axis=1)
    left_x = jnp.where(c == x // 2, left_x, lax.ppermute(left_x, "c", SWAP))
    mine = lax.dynamic_slice_in_dim(left_x, c * 2, 2, 0)
    below = jnp.concatenate(pieces(share), axis=1)
    below = jnp.pad(below, ((0, 15), (0, width - below.shape[1])))
    left = [jnp.concatenate([jnp.concatenate([mine[0], mine[1]], axis=1), below], axis=0)]
    held[1], other[0], across[0], across[1], right[2], left[0] = together(
        held[1], other[0], across[0], across[1], right[2], left[0]
    )

    held.append(apart(held[1], "z", 1, -1))
    other.append(lax.ppermute(held[1], "c", SWAP))
    across[1] = apart(across[1], "x", 2, 2)
    right.append(apart(right[-1], "y", 1, -1))
    left.append(apart(left[0], "z", 1, -1))
    held[2], other[1], across[1], right[3], left[1] = together(held[2], other[1], across[1], right[3], left[1])

    held.append(apart(held[2], "z", 1, -1))
    other.append(lax.ppermute(held[2], "c", SWAP))
    right = jnp.concatenate(right, axis=0)
    right_a, right_b = [right[:, : first + 128]], [right[:, first + 128 :]]
    right_a.append(apart(right_a[-1], "x", 1, -1))
    right_b.append(apart(right_b[-1], "x", 1, -1))
    left.append(apart(left[1], "z", 1, -1))
    moved = [near, far, *across]
    part_a = base_part(place, held[0], other[0], held[2], other[2], weight, moved)
    held[3] = after(held[3], part_a[0])
    right_a[1] = after(right_a[1], part_a[0])
    right_b[1] = after(right_b[1], part_a[0])
    other.append(lax.ppermute(held[3], "c", SWAP))
    right_a.append(apart(right_a[-1], "x", 1, -1))
    right_b.append(apart(right_b[-1], "x", 1, -1))

    part_b = base_part(place, held[1], other[3], held[3], other[1], weight, moved)
    right_a[2] = after(right_a[2], part_b[0])
    right_b[2] = after(right_b[2], part_b[0])
    right_a.append(apart(right_a[-1], "x", 1, -1))
    right_b.append(apart(right_b[-1], "x", 1, -1))
    left[2] = after(left[2], part_b[0])
    left.append(apart(left[2], "z", 1, -1))

    def onward(total, part):
        return (apart(total, "y", 1, -1).astype(F32) + part.astype(F32)).astype(BF16)

    def across_x(total):
        return jnp.stack([total[0]] + [shift(total[d], "x", -d) for d in range(1, 4)])

    sum_a = onward(part_a[0], part_a[1])
    sum_b = onward(part_b[0], part_b[1])
    sum_a = onward(sum_a, part_a[2])
    sum_b = onward(sum_b, part_b[2])
    sum_a = onward(sum_a, part_a[3])
    left[3], sum_a = together(left[3], sum_a)
    columns_a = across_x(sum_a)
    left_other = lax.ppermute(jnp.stack(left), "c", SWAP)
    sum_b = after(onward(sum_b, part_b[3]), columns_a, left_other)
    columns = jnp.concatenate([columns_a, across_x(sum_b)], axis=1)

    shares = jnp.stack([v[members, : 6 * members] for v in left])
    shares = jnp.concatenate([shares, left_other[:, members, : 6 * members]]).astype(F32)
    share = jnp.sum(shares, axis=0).reshape(3, 2 * members)
    probe = jnp.sum(share, axis=0).reshape(2 * members, 1) * (noise_scale / math.sqrt(features))
    outputs = output_part(place, columns, probe, right_factors)
    update = update_part(place, left, left_other, right_a, right_a, first, out_cols, 0, first)
    update = update_part(place, left, left_other, right_b, right_a, first, out_cols, first, out_cols - first, update)
    return outputs, update


def solution(mesh):
    grid = Mesh(mesh.devices.reshape(4, 4, 4, 2), ("y", "x", "z", "c"))
    spec = P(("y", "x"), ("z", "c"))
    return jax.shard_map(
        body,
        mesh=grid,
        in_specs=(spec, spec, spec, spec, P(("y", "x"))),
        out_specs=(spec, spec),
        check_vma=False,
    )
```

```python
import math

import jax
import jax.numpy as jnp
from jax import lax
from jax.experimental import pallas as pl
from jax.experimental.pallas import tpu as pltpu
from jax.sharding import Mesh, PartitionSpec as P

noise_scale = 0.5
epsilon = 1e-05
F32, BF16 = jnp.float32, jnp.bfloat16
VMEM = 60 * 2**20
SWAP = [(0, 1), (1, 0)]


def shift(value, axis, by):
    return lax.ppermute(value, axis, [(i, (i + by) % 4) for i in range(4)])


def apart(value, axis, up, down):
    perm = [(2 * i, 2 * ((i + up) % 4)) for i in range(4)]
    perm += [(2 * i + 1, 2 * ((i + down) % 4) + 1) for i in range(4)]
    return lax.ppermute(value, (axis, "c"), perm)


def after(value, *others):
    return lax.optimization_barrier((value, *others))[0]


def together(*values):
    return lax.optimization_barrier(values)


def pick(value, index):
    return lax.dynamic_index_in_dim(value, index, 0, keepdims=False)


def whole(shape):
    return pl.BlockSpec(shape, lambda i, s: (0,) * len(shape))


def base_kernel(s_ref, own0, other0, own1, other1, mine, near, far, across0, across1, *out_refs):
    nx, _, rows, _ = out_refs[0].shape
    ny = len(out_refs)
    depth = mine.shape[0]
    x, c = s_ref[1], s_ref[3]
    away = jnp.where(c == 0, 1, -1)
    low = depth // 2
    for k, (own, other) in enumerate(((own0, other0), (own1, other1))):
        total = None
        for piece, by, skip in (
            (mine, 0, 0), (near, -away, 0), (far, away, 0), (across0, 2, 0), (across1, 2, low)
        ):
            block = lax.rem(x + by + 4, 4)
            at = pl.ds(pl.multiple_of(lax.rem(block, 2) * depth + skip, 128), piece.shape[0])
            tok = jnp.where(lax.div(block, 2) == c, own[:, at], other[:, at])
            term = jnp.dot(tok, piece[...], preferred_element_type=F32)
            total = term if total is None else total + term
        total = total.astype(BF16)
        for d in range(nx):
            for s in range(ny):
                at = (d * ny + s) * rows
                out_refs[s][d, k] = total[at : at + rows]


def base_part(place, own0, other0, own1, other1, weight, moved):
    depth, cols = moved[0].shape
    height, width = own0.shape
    rows = height // 16
    return pl.pallas_call(
        base_kernel,
        grid_spec=pltpu.PrefetchScalarGridSpec(
            num_scalar_prefetch=1,
            grid=(1,),
            in_specs=[whole((height, width))] * 4
            + [pl.BlockSpec((depth, cols), lambda i, s: (0, s[1]))]
            + [whole(m.shape) for m in moved],
            out_specs=[whole((4, 2, rows, cols))] * 4,
        ),
        out_shape=[jax.ShapeDtypeStruct((4, 2, rows, cols), BF16)] * 4,
        compiler_params=pltpu.CompilerParams(vmem_limit_bytes=VMEM),
        cost_estimate=pl.CostEstimate(
            flops=16 * height * depth * cols,
            bytes_accessed=16 * height * depth + 4 * height * cols + 8 * depth * cols,
            transcendentals=0,
        ),
        name="base",
    )(place, own0, other0, own1, other1, weight, *moved)


def output_kernel(s_ref, *refs):
    sums, (probe_ref, right_ref, out_ref) = refs[:4], refs[4:]
    x, z, c = s_ref[1], s_ref[2], s_ref[3]
    _, rows, cols = sums[0].shape
    members = right_ref.shape[0]
    row = lax.broadcasted_iota(jnp.int32, (2 * members, members), 0)
    member = lax.broadcasted_iota(jnp.int32, (2 * members, members), 1)
    twice = jnp.where(lax.div(row, 2) == member, 1.0, 0.0).astype(BF16)
    for d in range(4):
        lanes = pl.ds(pl.multiple_of(lax.rem(x + d, 4) * cols, 128), cols)
        right = jnp.dot(twice, right_ref[:, lanes], preferred_element_type=F32)
        for zz in range(4):
            k = lax.rem(jnp.where(c == 0, z - zz, zz - z) + 4, 4)
            at = slice(zz * rows, (zz + 1) * rows)
            out = sums[d][lax.rem(k, 2) * 2 + lax.div(k, 2)].astype(F32)
            out_ref[at, lanes] = (out + probe_ref[at] * right[at]).astype(BF16)


def output_part(place, sums, probe, right):
    _, rows, cols = sums[0].shape
    out = (4 * rows, 4 * cols)
    return pl.pallas_call(
        output_kernel,
        grid_spec=pltpu.PrefetchScalarGridSpec(
            num_scalar_prefetch=1,
            grid=(1,),
            in_specs=[whole(v.shape) for v in (*sums, probe, right)],
            out_specs=whole(out),
        ),
        out_shape=jax.ShapeDtypeStruct(out, BF16),
        compiler_params=pltpu.CompilerParams(vmem_limit_bytes=VMEM),
        cost_estimate=pl.CostEstimate(flops=64 * 128 * out[1], bytes_accessed=8 * out[0] * out[1], transcendentals=0),
        name="outputs",
    )(place, *sums, probe, right)


def update_kernel(s_ref, left0, left1, left2, left3, left_other, *refs):
    *inputs, out_ref, ordered, turned, weighted, scores = refs
    rights, fits = inputs[: len(inputs) // 2], inputs[len(inputs) // 2 :]
    population, cols = ordered.shape

    @pl.when(pl.program_id(0) == 0)
    def _():
        z, c = s_ref[2], s_ref[3]
        count = population // 64
        for k, left in enumerate((left0, left1, left2, left3)):
            zz = lax.rem(jnp.where(c == 0, z - k, z + k) + 4, 4)
            for p in range(2):
                first = 2 * (c if p == 0 else 1 - c)
                for dd in range(2):
                    d = first + dd
                    d = jnp.where(c == 0, d, lax.rem(4 - d, 4))
                    for s in range(4):
                        slot = d * 4 + jnp.where(c == 0, s, -s % 4)
                        at = pl.multiple_of((slot * 4 + zz) * count, count)
                        rows, lanes = slice(s * count, (s + 1) * count), slice(dd * cols, (dd + 1) * cols)
                        ordered[pl.ds(at, count)] = left[rows, lanes] if p == 0 else left_other[-k % 4, rows, lanes]
        turned[...] = ordered[...].T
        fit = jnp.concatenate([f[...].astype(F32) for f in fits], axis=0)
        fit = fit[:, 0:1] + fit[:, 1:2] + fit[:, 2:3]
        mean = jnp.sum(fit, axis=0, keepdims=True) / population
        centred = fit - mean
        spread = jnp.sum(centred * centred, axis=0, keepdims=True) / population
        scores[...] = centred / jnp.sqrt(spread + epsilon)

    at = 0
    for right in rights:
        rows = slice(at, at + right.shape[0])
        weighted[rows] = (scores[rows] * right[...].astype(F32)).astype(BF16)
        at += right.shape[0]
    total = jnp.dot(turned[...], weighted[...], preferred_element_type=F32)
    out_ref[...] = (total * (1.0 / math.sqrt(population))).astype(BF16)


def update_part(place, left, left_other, rights, out_cols):
    population = sum(r.shape[0] for r in rights)
    depth = left[0].shape[1] // 2
    tile = 512
    return pl.pallas_call(
        update_kernel,
        grid_spec=pltpu.PrefetchScalarGridSpec(
            num_scalar_prefetch=1,
            grid=(out_cols // tile,),
            in_specs=[whole(left[0].shape)] * 4
            + [whole(left_other.shape)]
            + [pl.BlockSpec((r.shape[0], tile), lambda i, s: (0, i)) for r in rights]
            + [pl.BlockSpec((r.shape[0], 128), lambda i, s: (0, out_cols // 128)) for r in rights],
            out_specs=pl.BlockSpec((depth, tile), lambda i, s: (0, i)),
            scratch_shapes=[
                pltpu.VMEM((population, depth), BF16),
                pltpu.VMEM((depth, population), BF16),
                pltpu.VMEM((population, tile), BF16),
                pltpu.VMEM((population, 1), F32),
            ],
        ),
        out_shape=jax.ShapeDtypeStruct((depth, out_cols), BF16),
        compiler_params=pltpu.CompilerParams(vmem_limit_bytes=VMEM),
        cost_estimate=pl.CostEstimate(
            flops=2 * population * depth * out_cols,
            bytes_accessed=2 * (population * (out_cols + depth) + depth * out_cols),
            transcendentals=0,
        ),
        name="update",
    )(place, *left, left_other, *rights, *rights)


def pieces(value):
    out = []
    for _ in range(3):
        top = lax.reduce_precision(value, 8, 7)
        out.append(top.astype(BF16))
        value = value - top
    return out


def body(tokens, weight, left_factors, right_factors, fitness):
    y, x, z, c = (lax.axis_index(name) for name in ("y", "x", "z", "c"))
    place = jnp.stack([y, x, z, c]).astype(jnp.int32)
    members, width = left_factors.shape
    depth, out_cols = weight.shape
    quarter = out_cols // 4
    features = width * 8
    population = members * 16
    rows = tokens.shape[0] // 4

    half = width // 2

    beside = jnp.stack(pieces(fitness), axis=1)
    beside = jnp.pad(beside, ((0, 0), (0, 128 - beside.shape[1])))
    right = [jnp.concatenate([right_factors, beside], axis=1)]

    away = jnp.where(c == 0, 1, -1)

    def cols_of(source, xx):
        return lax.dynamic_slice_in_dim(source, (xx % 4) * quarter, quarter, 1)

    both = jnp.concatenate(
        [tokens.reshape(4, rows, width), left_factors.reshape(4, members // 4, width)], axis=1
    )
    own = pick(both, z)
    by_z = [own] + [shift(pick(both, (z + d) % 4), "z", d) for d in range(1, 4)]
    by_z = jnp.stack(by_z)
    near = apart(cols_of(after(weight, own), x + away), "x", 1, -1)
    by_z, weight, right[0] = together(by_z, weight, right[0])

    by_y = [pick(by_z, (z - y) % 4)] + [shift(pick(by_z, (z - y - d) % 4), "y", d) for d in range(1, 4)]
    by_y = jnp.stack(by_y)
    by_y, near, weight, right[0] = together(by_y, near, weight, right[0])

    tok_y = by_y[:, :rows].reshape(4 * rows, width)
    left_y = by_y[:, rows:].reshape(members, width)

    def left_for(xx):
        cols = lax.dynamic_slice_in_dim(left_y, (xx % 2) * half, half, 1)
        return jnp.concatenate([cols[: members // 2], cols[members // 2 :]], axis=1)

    slots = []
    for d in range(4):
        sent = jnp.concatenate([tok_y, left_for((x + d) % 4)], axis=0)
        slots.append(sent if d == 0 else shift(sent, "x", d))
    slots = jnp.stack(slots)
    far = apart(cols_of(weight, x - away), "x", -1, 1)
    right.append(apart(right[-1], "y", 1, -1))
    share = jnp.einsum(
        "mtd,md->mt", tokens.reshape(members, 2, width), left_factors, preferred_element_type=F32
    ).reshape(1, 2 * members)
    slots, share, right[1], weight = together(slots, share, right[1], weight)

    held = [slots[:, : 4 * rows].reshape(16 * rows, width)]
    held.append(apart(held[0], "z", 1, -1))
    other = [lax.ppermute(held[0], "c", SWAP)]
    across = cols_of(weight, x + 2)
    across = [apart(across[: depth // 2], "x", 2, 2), across[depth // 2 :]]
    right.append(apart(right[-1], "y", 1, -1))
    left_x = slots[:, 4 * rows :]
    left_x = jnp.concatenate([left_x[..., :half], left_x[..., half:]], axis=1)
    left_x = jnp.where(c == x // 2, left_x, lax.ppermute(left_x, "c", SWAP))
    mine = lax.dynamic_slice_in_dim(left_x, c * 2, 2, 0)
    below = jnp.concatenate(pieces(share), axis=1)
    below = jnp.pad(below, ((0, 15), (0, width - below.shape[1])))
    left = [jnp.concatenate([jnp.concatenate([mine[0], mine[1]], axis=1), below], axis=0)]
    held[1], other[0], far, across[0], across[1], right[2], left[0] = together(
        held[1], other[0], far, across[0], across[1], right[2], left[0]
    )

    held.append(apart(held[1], "z", 1, -1))
    other.append(lax.ppermute(held[1], "c", SWAP))
    across[1] = apart(across[1], "x", 2, 2)
    right.append(apart(right[-1], "y", 1, -1))
    held[2], other[1], across[1], right[3], left[0] = together(held[2], other[1], across[1], right[3], left[0])

    held.append(apart(held[2], "z", 1, -1))
    other.append(lax.ppermute(held[2], "c", SWAP))
    right = [jnp.concatenate(right, axis=0)]
    right.append(apart(right[-1], "x", 1, -1))
    moved = [near, far, *across]
    part_a = base_part(place, held[0], other[0], held[2], other[2], weight, moved)
    held[3], *part_a = together(held[3], *part_a)
    other.append(lax.ppermute(held[3], "c", SWAP))

    def along_y(part):
        return [part[0]] + [shift(part[-d], "y", d) for d in range(1, 4)]

    def total_of(terms):
        return sum(t.astype(F32) for t in terms[1:]) + terms[0].astype(F32)

    terms_a = along_y(part_a)
    right[1], other[3] = together(right[1], other[3])
    right.append(apart(right[-1], "x", 1, -1))
    part_b = base_part(place, held[1], other[3], held[3], other[1], weight, moved)
    terms_a[0], left[0], _ = together(terms_a[0], left[0], part_b[0])
    sum_a = total_of(terms_a).astype(BF16)
    sum_a, right[2], left[0], *part_b = together(sum_a, right[2], left[0], *part_b)
    right.append(apart(right[-1], "x", 1, -1))
    terms_b = along_y(part_b)
    for _ in range(3):
        left.append(apart(left[-1], "z", 1, -1))
    sum_b = total_of(terms_b).astype(BF16)
    sum_b, left[3], right[3] = together(sum_b, left[3], right[3])
    left_other = lax.ppermute(jnp.stack(left), "c", SWAP)

    total = jnp.concatenate([sum_a, sum_b], axis=1)
    columns = [total[0]] + [shift(total[d], "x", -d) for d in range(1, 4)]

    shares = jnp.stack([v[members, : 6 * members] for v in left])
    shares = jnp.concatenate([shares, left_other[:, members, : 6 * members]]).astype(F32)
    share = jnp.sum(shares, axis=0).reshape(3, 2 * members)
    probe = jnp.sum(share, axis=0).reshape(2 * members, 1) * (noise_scale / math.sqrt(features))
    left_other, columns[0], probe = together(left_other, columns[0], probe)
    update = update_part(place, left, left_other, right, out_cols)
    update, *columns = together(update, *columns)
    outputs = output_part(place, columns, probe, right_factors)
    return outputs, update


def solution(mesh):
    grid = Mesh(mesh.devices.reshape(4, 4, 4, 2), ("y", "x", "z", "c"))
    spec = P(("y", "x"), ("z", "c"))
    return jax.shard_map(
        body,
        mesh=grid,
        in_specs=(spec, spec, spec, spec, P(("y", "x"))),
        out_specs=(spec, spec),
        check_vma=False,
    )
```

```python
import math

import jax
import jax.numpy as jnp
from jax import lax
from jax.experimental import pallas as pl
from jax.experimental.pallas import tpu as pltpu
from jax.sharding import Mesh, PartitionSpec as P

noise_scale = 0.5
epsilon = 1e-05
F32, BF16 = jnp.float32, jnp.bfloat16
VMEM = 60 * 2**20
SWAP = [(0, 1), (1, 0)]


def shift(value, axis, by):
    return lax.ppermute(value, axis, [(i, (i + by) % 4) for i in range(4)])


def apart(value, axis, up, down):
    perm = [(2 * i, 2 * ((i + up) % 4)) for i in range(4)]
    perm += [(2 * i + 1, 2 * ((i + down) % 4) + 1) for i in range(4)]
    return lax.ppermute(value, (axis, "c"), perm)


def after(value, *others):
    return lax.optimization_barrier((value, *others))[0]


def together(*values):
    return lax.optimization_barrier(values)


def pick(value, index):
    return lax.dynamic_index_in_dim(value, index, 0, keepdims=False)


def whole(shape):
    return pl.BlockSpec(shape, lambda i, s: (0,) * len(shape))


def base_kernel(s_ref, own0, other0, own1, other1, mine, near, far, across0, across1, *out_refs):
    nx, _, rows, _ = out_refs[0].shape
    ny = len(out_refs)
    depth = mine.shape[0]
    x, c = s_ref[1], s_ref[3]
    away = jnp.where(c == 0, 1, -1)
    low = depth // 2
    for k, (own, other) in enumerate(((own0, other0), (own1, other1))):
        total = None
        for piece, by, skip in (
            (mine, 0, 0), (near, -away, 0), (far, away, 0), (across0, 2, 0), (across1, 2, low)
        ):
            block = lax.rem(x + by + 4, 4)
            at = pl.ds(pl.multiple_of(lax.rem(block, 2) * depth + skip, 128), piece.shape[0])
            tok = jnp.where(lax.div(block, 2) == c, own[:, at], other[:, at])
            term = jnp.dot(tok, piece[...], preferred_element_type=F32)
            total = term if total is None else total + term
        total = total.astype(BF16)
        for d in range(nx):
            for s in range(ny):
                at = (d * ny + s) * rows
                out_refs[s][d, k] = total[at : at + rows]


def base_part(place, own0, other0, own1, other1, weight, moved):
    depth, cols = moved[0].shape
    height, width = own0.shape
    rows = height // 16
    return pl.pallas_call(
        base_kernel,
        grid_spec=pltpu.PrefetchScalarGridSpec(
            num_scalar_prefetch=1,
            grid=(1,),
            in_specs=[whole((height, width))] * 4
            + [pl.BlockSpec((depth, cols), lambda i, s: (0, s[1]))]
            + [whole(m.shape) for m in moved],
            out_specs=[whole((4, 2, rows, cols))] * 4,
        ),
        out_shape=[jax.ShapeDtypeStruct((4, 2, rows, cols), BF16)] * 4,
        compiler_params=pltpu.CompilerParams(vmem_limit_bytes=VMEM),
        cost_estimate=pl.CostEstimate(
            flops=16 * height * depth * cols,
            bytes_accessed=16 * height * depth + 4 * height * cols + 8 * depth * cols,
            transcendentals=0,
        ),
        name="base",
    )(place, own0, other0, own1, other1, weight, *moved)


def output_kernel(s_ref, *refs):
    sums, (probe_ref, right_ref, out_ref) = refs[:4], refs[4:]
    x, z, c = s_ref[1], s_ref[2], s_ref[3]
    _, rows, cols = sums[0].shape
    members = right_ref.shape[0]
    row = lax.broadcasted_iota(jnp.int32, (2 * members, members), 0)
    member = lax.broadcasted_iota(jnp.int32, (2 * members, members), 1)
    twice = jnp.where(lax.div(row, 2) == member, 1.0, 0.0).astype(BF16)
    for d in range(4):
        lanes = pl.ds(pl.multiple_of(lax.rem(x + d, 4) * cols, 128), cols)
        right = jnp.dot(twice, right_ref[:, lanes], preferred_element_type=F32)
        for zz in range(4):
            k = lax.rem(jnp.where(c == 0, z - zz, zz - z) + 4, 4)
            at = slice(zz * rows, (zz + 1) * rows)
            out = sums[d][lax.rem(k, 2) * 2 + lax.div(k, 2)].astype(F32)
            out_ref[at, lanes] = (out + probe_ref[at, 0:1] * right[at]).astype(BF16)


def output_part(place, sums, probe, right):
    _, rows, cols = sums[0].shape
    out = (4 * rows, 4 * cols)
    return pl.pallas_call(
        output_kernel,
        grid_spec=pltpu.PrefetchScalarGridSpec(
            num_scalar_prefetch=1,
            grid=(1,),
            in_specs=[whole(v.shape) for v in (*sums, probe, right)],
            out_specs=whole(out),
        ),
        out_shape=jax.ShapeDtypeStruct(out, BF16),
        compiler_params=pltpu.CompilerParams(vmem_limit_bytes=VMEM),
        cost_estimate=pl.CostEstimate(flops=64 * 128 * out[1], bytes_accessed=8 * out[0] * out[1], transcendentals=0),
        name="outputs",
    )(place, *sums, probe, right)


def update_kernel(s_ref, left0, left1, left2, left3, left_other, *refs):
    *inputs, out_ref, ordered, turned, weighted, scores = refs
    rights, fits = inputs[: len(inputs) // 2], inputs[len(inputs) // 2 :]
    population, cols = ordered.shape

    @pl.when(pl.program_id(0) == 0)
    def _():
        z, c = s_ref[2], s_ref[3]
        count = population // 64
        for k, left in enumerate((left0, left1, left2, left3)):
            zz = lax.rem(jnp.where(c == 0, z - k, z + k) + 4, 4)
            for p in range(2):
                first = 2 * (c if p == 0 else 1 - c)
                for dd in range(2):
                    d = first + dd
                    d = jnp.where(c == 0, d, lax.rem(4 - d, 4))
                    for s in range(4):
                        slot = d * 4 + jnp.where(c == 0, s, -s % 4)
                        at = pl.multiple_of((slot * 4 + zz) * count, count)
                        rows, lanes = slice(s * count, (s + 1) * count), slice(dd * cols, (dd + 1) * cols)
                        ordered[pl.ds(at, count)] = left[rows, lanes] if p == 0 else left_other[-k % 4, rows, lanes]
        turned[...] = ordered[...].T
        fit = jnp.concatenate([f[...].astype(F32) for f in fits], axis=0)
        fit = fit[:, 0:1] + fit[:, 1:2] + fit[:, 2:3]
        mean = jnp.sum(fit, axis=0, keepdims=True) / population
        centred = fit - mean
        spread = jnp.sum(centred * centred, axis=0, keepdims=True) / population
        scores[...] = centred / jnp.sqrt(spread + epsilon)

    at = 0
    for right in rights:
        rows = slice(at, at + right.shape[0])
        weighted[rows] = (scores[rows] * right[...].astype(F32)).astype(BF16)
        at += right.shape[0]
    total = jnp.dot(turned[...], weighted[...], preferred_element_type=F32)
    out_ref[...] = (total * (1.0 / math.sqrt(population))).astype(BF16)


def update_part(place, left, left_other, rights, out_cols):
    population = sum(r.shape[0] for r in rights)
    depth = left[0].shape[1] // 2
    tile = 896
    return pl.pallas_call(
        update_kernel,
        grid_spec=pltpu.PrefetchScalarGridSpec(
            num_scalar_prefetch=1,
            grid=(out_cols // tile,),
            in_specs=[whole(left[0].shape)] * 4
            + [whole(left_other.shape)]
            + [pl.BlockSpec((r.shape[0], tile), lambda i, s: (0, i)) for r in rights]
            + [pl.BlockSpec((r.shape[0], 128), lambda i, s: (0, out_cols // 128)) for r in rights],
            out_specs=pl.BlockSpec((depth, tile), lambda i, s: (0, i)),
            scratch_shapes=[
                pltpu.VMEM((population, depth), BF16),
                pltpu.VMEM((depth, population), BF16),
                pltpu.VMEM((population, tile), BF16),
                pltpu.VMEM((population, 1), F32),
            ],
        ),
        out_shape=jax.ShapeDtypeStruct((depth, out_cols), BF16),
        compiler_params=pltpu.CompilerParams(vmem_limit_bytes=VMEM),
        cost_estimate=pl.CostEstimate(
            flops=2 * population * depth * out_cols,
            bytes_accessed=2 * (population * (out_cols + depth) + depth * out_cols),
            transcendentals=0,
        ),
        name="update",
    )(place, *left, left_other, *rights, *rights)


def pieces(value):
    out = []
    for _ in range(3):
        top = lax.reduce_precision(value, 8, 7)
        out.append(top.astype(BF16))
        value = value - top
    return out


def body(tokens, weight, left_factors, right_factors, fitness):
    y, x, z, c = (lax.axis_index(name) for name in ("y", "x", "z", "c"))
    place = jnp.stack([y, x, z, c]).astype(jnp.int32)
    members, width = left_factors.shape
    depth, out_cols = weight.shape
    quarter = out_cols // 4
    features = width * 8
    population = members * 16
    rows = tokens.shape[0] // 4

    half = width // 2

    beside = jnp.stack(pieces(fitness), axis=1)
    beside = jnp.pad(beside, ((0, 0), (0, 128 - beside.shape[1])))
    right = [jnp.concatenate([right_factors, beside], axis=1)]

    away = jnp.where(c == 0, 1, -1)

    def cols_of(source, xx):
        return lax.dynamic_slice_in_dim(source, (xx % 4) * quarter, quarter, 1)

    both = jnp.concatenate(
        [tokens.reshape(4, rows, width), left_factors.reshape(4, members // 4, width)], axis=1
    )
    own = pick(both, z)
    by_z = [own] + [shift(pick(both, (z + d) % 4), "z", d) for d in range(1, 4)]
    by_z = jnp.stack(by_z)
    near = apart(cols_of(after(weight, own), x + away), "x", 1, -1)
    by_z, weight, right[0] = together(by_z, weight, right[0])

    by_y = [pick(by_z, (z - y) % 4)] + [shift(pick(by_z, (z - y - d) % 4), "y", d) for d in range(1, 4)]
    by_y = jnp.stack(by_y)
    by_y, near, weight, right[0] = together(by_y, near, weight, right[0])

    tok_y = by_y[:, :rows].reshape(4 * rows, width)
    left_y = by_y[:, rows:].reshape(members, width)

    def left_for(xx):
        cols = lax.dynamic_slice_in_dim(left_y, (xx % 2) * half, half, 1)
        return jnp.concatenate([cols[: members // 2], cols[members // 2 :]], axis=1)

    slots = []
    for d in range(4):
        sent = jnp.concatenate([tok_y, left_for((x + d) % 4)], axis=0)
        slots.append(sent if d == 0 else shift(sent, "x", d))
    slots = jnp.stack(slots)
    far = apart(cols_of(weight, x - away), "x", -1, 1)
    right.append(apart(right[-1], "y", 1, -1))
    share = jnp.einsum(
        "mtd,md->mt", tokens.reshape(members, 2, width), left_factors, preferred_element_type=F32
    ).reshape(1, 2 * members)
    slots, share, right[1], weight = together(slots, share, right[1], weight)

    held = [slots[:, : 4 * rows].reshape(16 * rows, width)]
    held.append(apart(held[0], "z", 1, -1))
    other = [lax.ppermute(held[0], "c", SWAP)]
    across = cols_of(weight, x + 2)
    across = [apart(across[: depth // 2], "x", 2, 2), across[depth // 2 :]]
    right.append(apart(right[-1], "y", 1, -1))
    left_x = slots[:, 4 * rows :]
    left_x = jnp.concatenate([left_x[..., :half], left_x[..., half:]], axis=1)
    left_x = jnp.where(c == x // 2, left_x, lax.ppermute(left_x, "c", SWAP))
    mine = lax.dynamic_slice_in_dim(left_x, c * 2, 2, 0)
    below = jnp.concatenate(pieces(share), axis=1)
    below = jnp.pad(below, ((0, 15), (0, width - below.shape[1])))
    left = [jnp.concatenate([jnp.concatenate([mine[0], mine[1]], axis=1), below], axis=0)]
    held[1], other[0], far, across[0], across[1], right[2], left[0] = together(
        held[1], other[0], far, across[0], across[1], right[2], left[0]
    )

    held.append(apart(held[1], "z", 1, -1))
    other.append(lax.ppermute(held[1], "c", SWAP))
    across[1] = apart(across[1], "x", 2, 2)
    right.append(apart(right[-1], "y", 1, -1))
    held[2], other[1], across[1], left[0] = together(held[2], other[1], across[1], left[0])

    held.append(apart(held[2], "z", 1, -1))
    other.append(lax.ppermute(held[2], "c", SWAP))
    right = [jnp.concatenate(right, axis=0)]
    right.append(apart(right[-1], "x", 1, -1))
    moved = [near, far, *across]
    part_a = base_part(place, held[0], other[0], held[2], other[2], weight, moved)
    held[3], *part_a = together(held[3], *part_a)
    other.append(lax.ppermute(held[3], "c", SWAP))

    def along_y(part):
        return [part[0]] + [shift(part[-d], "y", d) for d in range(1, 4)]

    def total_of(terms):
        return sum(t.astype(F32) for t in terms[1:]) + terms[0].astype(F32)

    terms_a = along_y(part_a)
    right[1], other[3] = together(right[1], other[3])
    right.append(apart(right[-1], "x", 1, -1))
    part_b = base_part(place, held[1], other[3], held[3], other[1], weight, moved)
    terms_a[0], left[0], _ = together(terms_a[0], left[0], part_b[0])
    sum_a = total_of(terms_a).astype(BF16)
    sum_a, right[2], left[0] = together(sum_a, right[2], left[0])
    right.append(apart(right[-1], "x", 1, -1))
    terms_b = along_y(part_b)
    for _ in range(3):
        left.append(apart(left[-1], "z", 1, -1))
    sum_b = total_of(terms_b).astype(BF16)
    sum_b, left[3] = together(sum_b, left[3])
    left_other = lax.ppermute(jnp.stack(left), "c", SWAP)

    total = jnp.concatenate([sum_a, sum_b], axis=1)
    columns = [total[0]] + [shift(total[d], "x", -d) for d in range(1, 4)]

    shares = jnp.stack([v[members, : 6 * members] for v in left])
    shares = jnp.concatenate([shares, left_other[:, members, : 6 * members]]).astype(F32)
    share = jnp.sum(shares, axis=0).reshape(3, 2 * members)
    probe = jnp.sum(share, axis=0).reshape(2 * members, 1) * (noise_scale / math.sqrt(features))
    probe = jnp.broadcast_to(probe, (2 * members, 128))
    right[3], left_other, columns[0], probe = together(right[3], left_other, columns[0], probe)
    update = update_part(place, left, left_other, right, out_cols)
    update, *columns = together(update, *columns)
    outputs = output_part(place, columns, probe, right_factors)
    return outputs, update


def solution(mesh):
    grid = Mesh(mesh.devices.reshape(4, 4, 4, 2), ("y", "x", "z", "c"))
    spec = P(("y", "x"), ("z", "c"))
    return jax.shard_map(
        body,
        mesh=grid,
        in_specs=(spec, spec, spec, spec, P(("y", "x"))),
        out_specs=(spec, spec),
        check_vma=False,
    )
```

```python
import math

import jax
import jax.numpy as jnp
from jax import lax
from jax.experimental import pallas as pl
from jax.experimental.pallas import tpu as pltpu
from jax.sharding import Mesh, PartitionSpec as P

noise_scale = 0.5
epsilon = 1e-05
F32, BF16 = jnp.float32, jnp.bfloat16
VMEM = 60 * 2**20
SWAP = [(0, 1), (1, 0)]


def shift(value, axis, by):
    return lax.ppermute(value, axis, [(i, (i + by) % 4) for i in range(4)])


def apart(value, axis, up, down):
    perm = [(2 * i, 2 * ((i + up) % 4)) for i in range(4)]
    perm += [(2 * i + 1, 2 * ((i + down) % 4) + 1) for i in range(4)]
    return lax.ppermute(value, (axis, "c"), perm)


def after(value, *others):
    return lax.optimization_barrier((value, *others))[0]


def together(*values):
    return lax.optimization_barrier(values)


def pick(value, index):
    return lax.dynamic_index_in_dim(value, index, 0, keepdims=False)


def whole(shape):
    return pl.BlockSpec(shape, lambda i, s: (0,) * len(shape))


def base_kernel(s_ref, own0, other0, own1, other1, mine, near, far, across0, across1, *out_refs):
    nx, _, rows, _ = out_refs[0].shape
    ny = len(out_refs)
    depth = mine.shape[0]
    x, c = s_ref[1], s_ref[3]
    away = jnp.where(c == 0, 1, -1)
    low = depth // 2
    for k, (own, other) in enumerate(((own0, other0), (own1, other1))):
        total = None
        for piece, by, skip in (
            (mine, 0, 0), (near, -away, 0), (far, away, 0), (across0, 2, 0), (across1, 2, low)
        ):
            block = lax.rem(x + by + 4, 4)
            at = pl.ds(pl.multiple_of(lax.rem(block, 2) * depth + skip, 128), piece.shape[0])
            tok = jnp.where(lax.div(block, 2) == c, own[:, at], other[:, at])
            term = jnp.dot(tok, piece[...], preferred_element_type=F32)
            total = term if total is None else total + term
        total = total.astype(BF16)
        for d in range(nx):
            for s in range(ny):
                at = (d * ny + s) * rows
                out_refs[s][d, k] = total[at : at + rows]


def base_part(place, own0, other0, own1, other1, weight, moved):
    depth, cols = moved[0].shape
    height, width = own0.shape
    rows = height // 16
    return pl.pallas_call(
        base_kernel,
        grid_spec=pltpu.PrefetchScalarGridSpec(
            num_scalar_prefetch=1,
            grid=(1,),
            in_specs=[whole((height, width))] * 4
            + [pl.BlockSpec((depth, cols), lambda i, s: (0, s[1]))]
            + [whole(m.shape) for m in moved],
            out_specs=[whole((4, 2, rows, cols))] * 4,
        ),
        out_shape=[jax.ShapeDtypeStruct((4, 2, rows, cols), BF16)] * 4,
        compiler_params=pltpu.CompilerParams(vmem_limit_bytes=VMEM),
        cost_estimate=pl.CostEstimate(
            flops=16 * height * depth * cols,
            bytes_accessed=16 * height * depth + 4 * height * cols + 8 * depth * cols,
            transcendentals=0,
        ),
        name="base",
    )(place, own0, other0, own1, other1, weight, *moved)


def output_kernel(s_ref, *refs):
    sums, (probe_ref, right_ref, out_ref) = refs[:4], refs[4:]
    x, z, c = s_ref[1], s_ref[2], s_ref[3]
    _, rows, cols = sums[0].shape
    members = right_ref.shape[0]
    row = lax.broadcasted_iota(jnp.int32, (2 * members, members), 0)
    member = lax.broadcasted_iota(jnp.int32, (2 * members, members), 1)
    twice = jnp.where(lax.div(row, 2) == member, 1.0, 0.0).astype(BF16)
    for d in range(4):
        lanes = pl.ds(pl.multiple_of(lax.rem(x + d, 4) * cols, 128), cols)
        right = jnp.dot(twice, right_ref[:, lanes], preferred_element_type=F32)
        for zz in range(4):
            k = lax.rem(jnp.where(c == 0, z - zz, zz - z) + 4, 4)
            at = slice(zz * rows, (zz + 1) * rows)
            out = sums[d][lax.rem(k, 2) * 2 + lax.div(k, 2)].astype(F32)
            out_ref[at, lanes] = (out + probe_ref[at, 0:1] * right[at]).astype(BF16)


def output_part(place, sums, probe, right):
    _, rows, cols = sums[0].shape
    out = (4 * rows, 4 * cols)
    return pl.pallas_call(
        output_kernel,
        grid_spec=pltpu.PrefetchScalarGridSpec(
            num_scalar_prefetch=1,
            grid=(1,),
            in_specs=[whole(v.shape) for v in (*sums, probe, right)],
            out_specs=whole(out),
        ),
        out_shape=jax.ShapeDtypeStruct(out, BF16),
        compiler_params=pltpu.CompilerParams(vmem_limit_bytes=VMEM),
        cost_estimate=pl.CostEstimate(flops=64 * 128 * out[1], bytes_accessed=8 * out[0] * out[1], transcendentals=0),
        name="outputs",
    )(place, *sums, probe, right)


def update_kernel(s_ref, left0, left1, left2, left3, left_other, *refs):
    *inputs, out_ref, ordered, turned, weighted, scores = refs
    rights, fits = inputs[: len(inputs) // 2], inputs[len(inputs) // 2 :]
    population, cols = ordered.shape

    @pl.when(pl.program_id(0) == 0)
    def _():
        z, c = s_ref[2], s_ref[3]
        count = population // 64
        for k, left in enumerate((left0, left1, left2, left3)):
            zz = lax.rem(jnp.where(c == 0, z - k, z + k) + 4, 4)
            for p in range(2):
                first = 2 * (c if p == 0 else 1 - c)
                for dd in range(2):
                    d = first + dd
                    d = jnp.where(c == 0, d, lax.rem(4 - d, 4))
                    for s in range(4):
                        slot = d * 4 + jnp.where(c == 0, s, -s % 4)
                        at = pl.multiple_of((slot * 4 + zz) * count, count)
                        rows, lanes = slice(s * count, (s + 1) * count), slice(dd * cols, (dd + 1) * cols)
                        ordered[pl.ds(at, count)] = left[rows, lanes] if p == 0 else left_other[-k % 4, rows, lanes]
        turned[...] = ordered[...].T
        fit = jnp.concatenate([f[...].astype(F32) for f in fits], axis=0)
        fit = fit[:, 0:1] + fit[:, 1:2] + fit[:, 2:3]
        mean = jnp.sum(fit, axis=0, keepdims=True) / population
        centred = fit - mean
        spread = jnp.sum(centred * centred, axis=0, keepdims=True) / population
        scores[...] = centred / jnp.sqrt(spread + epsilon)

    at = 0
    for right in rights:
        rows = slice(at, at + right.shape[0])
        weighted[rows] = (scores[rows] * right[...].astype(F32)).astype(BF16)
        at += right.shape[0]
    total = jnp.dot(turned[...], weighted[...], preferred_element_type=F32)
    out_ref[...] = (total * (1.0 / math.sqrt(population))).astype(BF16)


def update_part(place, left, left_other, rights, out_cols):
    population = sum(r.shape[0] for r in rights)
    depth = left[0].shape[1] // 2
    tile = 896
    return pl.pallas_call(
        update_kernel,
        grid_spec=pltpu.PrefetchScalarGridSpec(
            num_scalar_prefetch=1,
            grid=(out_cols // tile,),
            in_specs=[whole(left[0].shape)] * 4
            + [whole(left_other.shape)]
            + [pl.BlockSpec((r.shape[0], tile), lambda i, s: (0, i)) for r in rights]
            + [pl.BlockSpec((r.shape[0], 128), lambda i, s: (0, out_cols // 128)) for r in rights],
            out_specs=pl.BlockSpec((depth, tile), lambda i, s: (0, i)),
            scratch_shapes=[
                pltpu.VMEM((population, depth), BF16),
                pltpu.VMEM((depth, population), BF16),
                pltpu.VMEM((population, tile), BF16),
                pltpu.VMEM((population, 1), F32),
            ],
        ),
        out_shape=jax.ShapeDtypeStruct((depth, out_cols), BF16),
        compiler_params=pltpu.CompilerParams(vmem_limit_bytes=VMEM),
        cost_estimate=pl.CostEstimate(
            flops=2 * population * depth * out_cols,
            bytes_accessed=2 * (population * (out_cols + depth) + depth * out_cols),
            transcendentals=0,
        ),
        name="update",
    )(place, *left, left_other, *rights, *rights)


def pieces(value):
    out = []
    for _ in range(3):
        top = lax.reduce_precision(value, 8, 7)
        out.append(top.astype(BF16))
        value = value - top
    return out


def body(tokens, weight, left_factors, right_factors, fitness):
    y, x, z, c = (lax.axis_index(name) for name in ("y", "x", "z", "c"))
    place = jnp.stack([y, x, z, c]).astype(jnp.int32)
    members, width = left_factors.shape
    depth, out_cols = weight.shape
    quarter = out_cols // 4
    features = width * 8
    population = members * 16
    rows = tokens.shape[0] // 4

    half = width // 2

    beside = jnp.stack(pieces(fitness), axis=1)
    beside = jnp.pad(beside, ((0, 0), (0, 128 - beside.shape[1])))
    right = [jnp.concatenate([right_factors, beside], axis=1)]

    away = jnp.where(c == 0, 1, -1)

    def cols_of(source, xx):
        return lax.dynamic_slice_in_dim(source, (xx % 4) * quarter, quarter, 1)

    both = jnp.concatenate(
        [tokens.reshape(4, rows, width), left_factors.reshape(4, members // 4, width)], axis=1
    )
    own = pick(both, z)
    by_z = [own] + [shift(pick(both, (z + d) % 4), "z", d) for d in range(1, 4)]
    by_z = jnp.stack(by_z)
    near = apart(cols_of(after(weight, own), x + away), "x", 1, -1)
    by_z, weight, right[0] = together(by_z, weight, right[0])

    by_y = [pick(by_z, (z - y) % 4)] + [shift(pick(by_z, (z - y - d) % 4), "y", d) for d in range(1, 4)]
    by_y = jnp.stack(by_y)
    by_y, near, weight, right[0] = together(by_y, near, weight, right[0])

    tok_y = by_y[:, :rows].reshape(4 * rows, width)
    left_y = by_y[:, rows:].reshape(members, width)

    def left_for(xx):
        cols = lax.dynamic_slice_in_dim(left_y, (xx % 2) * half, half, 1)
        return jnp.concatenate([cols[: members // 2], cols[members // 2 :]], axis=1)

    slots = []
    for d in range(4):
        sent = jnp.concatenate([tok_y, left_for((x + d) % 4)], axis=0)
        slots.append(sent if d == 0 else shift(sent, "x", d))
    slots = jnp.stack(slots)
    far = apart(cols_of(weight, x - away), "x", -1, 1)
    right.append(apart(right[-1], "y", 1, -1))
    share = jnp.einsum(
        "mtd,md->mt", tokens.reshape(members, 2, width), left_factors, preferred_element_type=F32
    ).reshape(1, 2 * members)
    slots, share, right[1], weight = together(slots, share, right[1], weight)

    held = [slots[:, : 4 * rows].reshape(16 * rows, width)]
    held.append(apart(held[0], "z", 1, -1))
    other = [lax.ppermute(held[0], "c", SWAP)]
    across = cols_of(weight, x + 2)
    across = [apart(across[: depth // 2], "x", 2, 2), across[depth // 2 :]]
    right.append(apart(right[-1], "y", 1, -1))
    left_x = slots[:, 4 * rows :]
    left_x = jnp.concatenate([left_x[..., :half], left_x[..., half:]], axis=1)
    left_x = jnp.where(c == x // 2, left_x, lax.ppermute(left_x, "c", SWAP))
    mine = lax.dynamic_slice_in_dim(left_x, c * 2, 2, 0)
    below = jnp.concatenate(pieces(share), axis=1)
    below = jnp.pad(below, ((0, 15), (0, width - below.shape[1])))
    left = [jnp.concatenate([jnp.concatenate([mine[0], mine[1]], axis=1), below], axis=0)]
    held[1], other[0], far, across[0], across[1], right[2], left[0] = together(
        held[1], other[0], far, across[0], across[1], right[2], left[0]
    )

    held.append(apart(held[1], "z", 1, -1))
    other.append(lax.ppermute(held[1], "c", SWAP))
    across[1] = apart(across[1], "x", 2, 2)
    right.append(apart(right[-1], "y", 1, -1))
    held[2], other[1], across[1], left[0] = together(held[2], other[1], across[1], left[0])

    held.append(apart(held[2], "z", 1, -1))
    other.append(lax.ppermute(held[2], "c", SWAP))
    right = [jnp.concatenate(right, axis=0)]
    right.append(apart(right[-1], "x", 1, -1))
    moved = [near, far, *across]
    part_a = base_part(place, held[0], other[0], held[2], other[2], weight, moved)
    held[3], *part_a = together(held[3], *part_a)
    other.append(lax.ppermute(held[3], "c", SWAP))

    def along_y(part):
        return [part[0]] + [shift(part[-d], "y", d) for d in range(1, 4)]

    def total_of(terms):
        return sum(t.astype(F32) for t in terms[1:]) + terms[0].astype(F32)

    terms_a = along_y(part_a)
    right[1], other[3] = together(right[1], other[3])
    right.append(apart(right[-1], "x", 1, -1))
    part_b = base_part(place, held[1], other[3], held[3], other[1], weight, moved)
    terms_a[0], left[0], _ = together(terms_a[0], left[0], part_b[0])
    sum_a = total_of(terms_a).astype(BF16)
    sum_a, right[2], left[0] = together(sum_a, right[2], left[0])
    right.append(apart(right[-1], "x", 1, -1))
    terms_b = along_y(part_b)
    for _ in range(3):
        left.append(apart(left[-1], "z", 1, -1))
    sum_b = total_of(terms_b).astype(BF16)
    sum_b, left[2] = together(sum_b, left[2])
    left_other = lax.ppermute(jnp.stack(left), "c", SWAP)

    total = jnp.concatenate([sum_a, sum_b], axis=1)
    columns = [total[0]] + [shift(total[d], "x", -d) for d in range(1, 4)]

    shares = jnp.stack([v[members, : 6 * members] for v in left])
    shares = jnp.concatenate([shares, left_other[:, members, : 6 * members]]).astype(F32)
    share = jnp.sum(shares, axis=0).reshape(3, 2 * members)
    probe = jnp.sum(share, axis=0).reshape(2 * members, 1) * (noise_scale / math.sqrt(features))
    probe = jnp.broadcast_to(probe, (2 * members, 128))
    right[3], left_other, columns[0], probe = together(right[3], left_other, columns[0], probe)
    update = update_part(place, left, left_other, right, out_cols)
    update, *columns = together(update, *columns)
    outputs = output_part(place, columns, probe, right_factors)
    return outputs, update


def solution(mesh):
    grid = Mesh(mesh.devices.reshape(4, 4, 4, 2), ("y", "x", "z", "c"))
    spec = P(("y", "x"), ("z", "c"))
    return jax.shard_map(
        body,
        mesh=grid,
        in_specs=(spec, spec, spec, spec, P(("y", "x"))),
        out_specs=(spec, spec),
        check_vma=False,
    )
```
